512 devices in a mesh: gx: 32 (over y, x_lo, core), gy: 16 (over z, x_hi).
Axes of the slice: x: 4 (x_hi: 2, x_lo: 2; x = x_hi * 2 + x_lo), y: 8, z: 8, core: 2. Of those that a mesh axis runs over, the one named last changes fastest.
Arguments:
- west_in: float32 [2, 128, 1024, 128], P(None, 'gx', 'gy'), may hold values from -6 to 6
- south_in: float32 [2, 1024, 64, 128], P(None, 'gx', 'gy'), may hold values from -6 to 6
- region: int32 [1024, 1024], P('gx', 'gy'), may hold values from 0 to 7
- pml_layers: int32 [4, 32, 16], P(None, 'gx', 'gy'), may hold values from 0 to 8
- vel_table: float32 [8, 128], replicated, may hold values from 0.3 to 3
- src_slot: int32 [32, 16], P('gx', 'gy'), may hold values from 0 to 48
- src_cell: int32 [32, 16], P('gx', 'gy'), may hold values from 0 to 262143
- src_amp: float32 [2, 49], replicated, may hold values from -16 to 16
- wave_sq: float32 [], replicated, may hold values from 0.5 to 2
Outputs:
- fields: bfloat16 [3, 2, 1024, 1024, 128], P(None, None, 'gx', 'gy')
The draws below stay inside these ranges and needn't reach their ends.
All inputs are finite; a program needn't handle non-finite values.
Results may differ from the reference program's by a relative error of at most 0.001.
Values sent between devices are 32-bit elements; how exact they have to be, the bound alone decides.
No kernel may reach another device: no remote copies, remote signals or barrier semaphores. Data moves between devices by JAX's collectives and lax.ppermute only.
A program may use at most 64 MiB of HBM per device.

```python
import math
import jax
import jax.numpy as jnp
from jax import lax

SX = 32
SY = 64
Z = 128
DEPTH = 4
TICKS = 3
REGIONS = 8
NX = 1024
NY = 1024
NSRC = 49
N_GX = 32
N_GY = 16


def draw_west_in(key, part):
    key_rough = jax.random.fold_in(jax.random.fold_in(key, 11), 0)
    blocks_x = NX // SX
    shape_all = (2, DEPTH * blocks_x, NY, Z)
    values = jax.random.normal(key_rough, shape_all, jnp.float32)
    return jnp.clip(values, -6.0, 6.0)


def draw_south_in(key, part):
    key_rough = jax.random.fold_in(jax.random.fold_in(key, 23), 0)
    blocks_y = NY // SY
    shape_all = (2, NX, DEPTH * blocks_y, Z)
    values = jax.random.normal(key_rough, shape_all, jnp.float32)
    return jnp.clip(values, -6.0, 6.0)


def draw_wave_sq(key, part):
    inner = jax.random.fold_in(key, 37)
    value = jax.random.uniform(inner, (), jnp.float32, 0.5, 2.0)
    return value


def place_ends(drawn, key, low, top_value):
    dims = drawn.shape
    index_at = [jax.random.randint(jax.random.fold_in(key, axis), (), 0, dims[axis]) for axis in range(len(dims))]
    drawn = drawn.at[tuple(index_at)].set(low)
    longest = dims.index(max(dims))
    index_at[longest] = (index_at[longest] + 1) % dims[longest]
    return drawn.at[tuple(index_at)].set(top_value)


def centred(own_key, dims, scale, bound, held_as=jnp.bfloat16):
    values = jax.random.normal(own_key, dims, jnp.float32) * scale
    return jnp.minimum(jnp.maximum(values, -bound), bound).astype(held_as)


def setup_inputs(seed: int = 0) -> dict:
    keys = jax.random.split(jax.random.key(seed), 10)
    west_in = draw_west_in(jax.random.fold_in(keys[9], 71), 0)
    south_in = draw_south_in(jax.random.fold_in(keys[9], 71), 0)
    region = place_ends(jax.random.randint(keys[2], (NX, NY), 0, REGIONS), jax.random.fold_in(keys[2], 1), 0, REGIONS - 1).astype(jnp.int32)
    pml_layers = place_ends(jax.random.randint(keys[3], (4, N_GX, N_GY), 0, 9), jax.random.fold_in(keys[3], 1), 0, 8).astype(jnp.int32)
    vel_table = jnp.clip(jnp.exp(jax.random.uniform(keys[4], (REGIONS, Z), jnp.float32, math.log(0.3), math.log(3.0))), 0.3, 3.0)
    src_slot = place_ends(jax.random.randint(keys[5], (N_GX, N_GY), 0, NSRC), jax.random.fold_in(keys[5], 1), 0, NSRC - 1).astype(jnp.int32)
    src_cell = place_ends(jax.random.randint(keys[6], (N_GX, N_GY), 0, SX * SY * Z), jax.random.fold_in(keys[6], 1), 0, (SX * SY * Z) - 1).astype(jnp.int32)
    src_amp = centred(keys[7], (2, NSRC), 4.0, 16.0, jnp.float32)
    wave_sq = draw_wave_sq(jax.random.fold_in(keys[9], 71), 0)
    return {"west_in": west_in, "south_in": south_in, "region": region, "pml_layers": pml_layers, "vel_table": vel_table, "src_slot": src_slot, "src_cell": src_cell, "src_amp": src_amp, "wave_sq": wave_sq}


precise_mode = lax.Precision.HIGHEST
damping_ratio = 0.25
absorb_peak = 4.0
diagonal_base = 6.0

def tables(count):
    index_vals = jnp.arange(count, dtype=jnp.float32)
    angle_grid = jnp.pi * (index_vals[:, None] + 1.0) * (index_vals[None, :] + 1.0) / (count + 1.0)
    basis_table = jnp.sqrt(2.0 / (count + 1.0)) * jnp.sin(angle_grid)
    eigen_vals = 2.0 - 2.0 * jnp.cos(jnp.pi * (index_vals + 1.0) / (count + 1.0))
    return (basis_table, eigen_vals)

def along_first(field, basis_table):
    return jnp.einsum('kx,cxyz->ckyz', basis_table, field, precision=precise_mode)

def along_second(field, basis_table):
    return jnp.einsum('ky,cxyz->cxkz', basis_table, field, precision=precise_mode)

def along_third(field, basis_table):
    return jnp.einsum('kz,cxyz->cxyk', basis_table, field, precision=precise_mode)

def spectral(forcing, wave_sq, bases):
    basis_x, eigen_x, basis_y, eigen_y, basis_z, eigen_z = bases
    coeffs = along_third(along_second(along_first(forcing, basis_x), basis_y), basis_z)
    shifted = eigen_x[:, None, None] + eigen_y[None, :, None] + eigen_z[None, None, :] - wave_sq
    damping = -damping_ratio * wave_sq
    denominator = shifted * shifted + damping * damping
    real_part = (coeffs[0] * shifted + coeffs[1] * damping) / denominator
    imag_part = (coeffs[1] * shifted - coeffs[0] * damping) / denominator
    return along_third(jnp.stack([real_part, imag_part]), basis_z)

def absorption(layers, size_x, size_y):
    first_pos = jnp.arange(size_x, dtype=jnp.float32)
    second_pos = jnp.arange(size_y, dtype=jnp.float32)

    def ramp(thick, distance):
        portion = jnp.maximum(thick - distance, 0.0) / jnp.maximum(thick, 1.0)
        return portion * portion
    sigma = ramp(layers[0], first_pos)[:, None] + ramp(layers[1], size_x - 1.0 - first_pos)[:, None]
    sigma = sigma + ramp(layers[2], second_pos)[None, :] + ramp(layers[3], size_y - 1.0 - second_pos)[None, :]
    return absorb_peak * sigma

def multipliers(speed_sq, sigma, wave_sq):
    contrast = speed_sq - wave_sq
    denominator = (diagonal_base * diagonal_base + sigma * sigma)[:, :, None]
    mult_real = contrast * diagonal_base / denominator
    mult_imag = -contrast * sigma[:, :, None] / denominator
    return (mult_real, mult_imag)

def correct(field, mult_real, mult_imag):
    real_part = field[0] + mult_real * field[0] - mult_imag * field[1]
    imag_part = field[1] + mult_real * field[1] + mult_imag * field[0]
    return jnp.stack([real_part, imag_part])

def cell_numbers(size_x, size_y, size_z):
    shape_all = (size_x, size_y, size_z)
    first_axis = lax.broadcasted_iota(jnp.int32, shape_all, 0)
    second_axis = lax.broadcasted_iota(jnp.int32, shape_all, 1)
    third_axis = lax.broadcasted_iota(jnp.int32, shape_all, 2)
    return (first_axis * size_y + second_axis) * size_z + third_axis

def build_forcing(west_trace, south_trace, amplitude, live, point_mask, size_x, size_y):
    west_pad = jnp.pad(west_trace, ((0, 0), (0, size_x - DEPTH), (0, 0), (0, 0)))
    south_pad = jnp.pad(south_trace, ((0, 0), (0, 0), (0, size_y - DEPTH), (0, 0)))
    return west_pad + south_pad + amplitude[:, :, None, None] * (live * point_mask)[None]

def block_tick(west_trace, south_trace, labels, layers, slot_value, cell_value, row_index, col_index, tick_index, vel_table, src_amp, wave_sq):
    bases = tables(SX) + tables(SY) + tables(Z)
    speed_sq = jnp.take(vel_table, labels, axis=0)
    sigma = absorption(layers.astype(jnp.float32), SX, SY)
    mult_real, mult_imag = multipliers(speed_sq, sigma, wave_sq)
    source_index = (tick_index - row_index - col_index + N_GX + N_GY - 2).astype(jnp.int32)
    live = (slot_value == source_index).astype(jnp.float32)
    point_mask = (cell_numbers(SX, SY, Z) == cell_value).astype(jnp.float32)
    amplitude = lax.dynamic_slice_in_dim(src_amp, source_index, 1, 1)
    forcing = build_forcing(west_trace, south_trace, amplitude, live, point_mask, SX, SY)
    partial_field = spectral(forcing, wave_sq, bases)
    raw_field = along_first(along_second(partial_field, bases[2]), bases[0])
    return correct(raw_field, mult_real, mult_imag)

def reference(west_in, south_in, region, pml_layers, vel_table, src_slot, src_cell, src_amp, wave_sq):
    west_traces = west_in.reshape(2, N_GX, DEPTH, N_GY, SY, Z).transpose(1, 3, 0, 2, 4, 5)
    south_traces = south_in.reshape(2, N_GX, SX, N_GY, DEPTH, Z).transpose(1, 3, 0, 2, 4, 5)
    label_blocks = region.reshape(N_GX, SX, N_GY, SY).transpose(0, 2, 1, 3)
    layer_blocks = pml_layers.transpose(1, 2, 0)
    row_ids = jnp.arange(N_GX, dtype=jnp.int32)
    col_ids = jnp.arange(N_GY, dtype=jnp.int32)
    results = []
    for tick_index in range(TICKS):

        def one_row(row_items):
            row_index, west_row, south_row, label_row, layer_row, slot_row, cell_row = row_items

            def one_block(col_index, west_block, south_block, label_block, layer_block, slot_value, cell_value):
                field = block_tick(west_block, south_block, label_block, layer_block, slot_value, cell_value, row_index, col_index, tick_index, vel_table, src_amp, wave_sq)
                return (field.astype(jnp.bfloat16), field[:, SX - DEPTH:], field[:, :, SY - DEPTH:])
            return jax.vmap(one_block)(col_ids, west_row, south_row, label_row, layer_row, slot_row, cell_row)
        blocks, east_part, north_part = lax.map(one_row, (row_ids, west_traces, south_traces, label_blocks, layer_blocks, src_slot, src_cell))
        results.append(blocks)
        west_traces = jnp.concatenate([jnp.zeros_like(east_part[:1]), east_part[:-1]], axis=0)
        south_traces = jnp.concatenate([jnp.zeros_like(north_part[:, :1]), north_part[:, :-1]], axis=1)
    stacked = jnp.stack(results)
    return stacked.transpose(0, 3, 1, 4, 2, 5, 6).reshape(TICKS, 2, N_GX * SX, N_GY * SY, Z)
```

```python
import functools

import jax
import jax.numpy as jnp
import ml_dtypes
import numpy as np
from jax import lax
from jax.experimental import pallas as pl
from jax.experimental.pallas import tpu as pltpu
from jax.sharding import PartitionSpec as P

DEPTH = 4
TICKS = 3
SUB = 8
GROUP = 4
DAMPING = 0.25
PEAK = 4.0
BASE = 6.0
F32 = jnp.float32
BF16 = jnp.bfloat16


def shift(array, axis):
    peers = lax.axis_size(axis)
    return lax.ppermute(array, axis, [(i, i + 1) for i in range(peers - 1)])


def basis(n):
    k = np.arange(1, n + 1, dtype=np.float64)
    table = np.sqrt(2.0 / (n + 1)) * np.sin(np.pi * np.outer(k, k) / (n + 1))
    return table, 2.0 - 2.0 * np.cos(np.pi * k / (n + 1))


def halves(table):
    high = table.astype(ml_dtypes.bfloat16)
    low = (table - high.astype(np.float64)).astype(ml_dtypes.bfloat16)
    return high, low


def stacked(table):
    high, low = halves(table)
    return np.block([[high, high], [low, np.zeros_like(low)]])


def constants(sx, sy, sz):
    bx, ex = basis(sx)
    by, ey = basis(sy)
    bz, ez = basis(sz)
    zh, zl = halves(bz)
    half = sx // 2
    eye = np.eye(SUB)
    narrow = {
        "z": np.block([[zh, zl], [zh, zl]]),
        "even": stacked(np.kron(bx[:half, 0::2], eye)),
        "odd": stacked(np.kron(bx[:half, 1::2], eye)),
        "y": stacked(by),
        "south": stacked(np.kron(bx, np.eye(DEPTH))),
        "west": np.concatenate(halves(np.kron(bx[order(sx), :DEPTH], eye)), axis=1),
    }
    wide = {
        "eigen": ey[:, None] + ez[None, :],
        "bx": bx,
        "by": by,
        "bz": bz,
        "reach": np.repeat(by[:, :DEPTH].T.reshape(DEPTH * sy, 1), sz, axis=1),
    }
    return pack(narrow, ml_dtypes.bfloat16), pack(wide, np.float32)


def order(sx):
    return list(range(0, sx, 2)) + list(range(1, sx, 2))


def pack(tables, dtype):
    width = max(t.shape[1] for t in tables.values())
    rows, places, at = [], {}, 0
    for name, t in tables.items():
        places[name] = (at, t.shape)
        rows.append(np.pad(t.astype(np.float64), ((0, 0), (0, width - t.shape[1]))))
        at += t.shape[0]
    return np.concatenate(rows).astype(dtype), places


def split(values):
    high = values.astype(BF16)
    low = (values - high.astype(F32)).astype(BF16)
    return high, low


def dot(a, b):
    return jnp.dot(a, b, preferred_element_type=F32)


def along_z(rows, z_table):
    high, low = split(rows)
    both = dot(jnp.concatenate([high, low], axis=1), z_table)
    size_z = rows.shape[1]
    return both[:, :size_z] + both[:, size_z:]


def from_left(table, rows):
    high, low = split(rows)
    both = dot(table, jnp.concatenate([high, low], axis=0))
    n = both.shape[0] // 2
    return both[:n] + both[n:]


def ramp(layers, distance):
    portion = jnp.maximum(layers - distance, 0.0) / jnp.maximum(layers, 1.0)
    return portion * portion


def point_rows(sizes, values, slot, cell, amp, wave, aux):
    sx, sy, sz = sizes
    bits = [size.bit_length() - 1 for size in sizes]
    number = cell[...]
    cell_x = lax.shift_right_logical(number, bits[1] + bits[2])
    cell_y = lax.shift_right_logical(number, bits[2]) & (sy - 1)
    cell_z = number & (sz - 1)

    def column(name, size, where):
        lane = lax.broadcasted_iota(jnp.int32, (size, sz), 1)
        return jnp.sum(jnp.where(lane == where, values(name, 0, size), 0.0), axis=1, keepdims=True)

    aux[:sy] = jnp.broadcast_to(column("by", sy, cell_y), (sy, sz))
    row = lax.broadcasted_iota(jnp.int32, (sz, sz), 0)
    bz_row = jnp.sum(jnp.where(row == cell_z, values("bz", 0, sz), 0.0), axis=0, keepdims=True)
    aux[sy : sy + sx] = column("bx", sx, cell_x) * bz_row
    first = lax.axis_size("gx") + lax.axis_size("gy") - 2 - lax.axis_index("gx") - lax.axis_index("gy")
    lane = lax.broadcasted_iota(jnp.int32, amp.shape, 1)
    at = sy + sx
    for tick in range(TICKS):
        strength = jnp.sum(jnp.where(lane == first + tick, amp[...], 0.0), axis=1, keepdims=True)
        strength = jnp.where(slot[...] == first + tick, strength, 0.0)
        aux[at + 2 * tick : at + 2 * tick + 2] = jnp.broadcast_to(strength, (2, sz))
    at += 2 * TICKS
    aux[at : at + 1] = jnp.broadcast_to(wave[...], (1, sz))


def aux_rows(sizes):
    sx, sy, _ = sizes
    return -(-(sx + sy + 2 * TICKS + 1) // SUB) * SUB


def tick_kernel(tick, sizes, places, *refs):
    sx, sy, sz = sizes
    refs = list(refs)
    take = lambda n: [refs.pop(0) for _ in range(n)]
    last = tick + 1 == TICKS
    fields = []
    if tick == 0:
        fetched = take(11)
        east, north, field, narrow, wide, aux, gain_re, gain_im = take(8)
    else:
        narrow, wide, aux, gain_re, gain_im, west, south = take(7)
        if last:
            fields = take(TICKS - 1)
            (out,) = take(1)
        else:
            east, north, field = take(3)
    west_hat, south_hat, grid = take(3)
    fetches = []
    if tick == 0:
        west, south, region, vel, layers, slot, cell, amp, wave = take(9)
        (fetch_sems,) = take(1)
        for i, target in enumerate([narrow, wide, west, south, region, vel, layers, slot, cell, amp, wave]):
            copy = pltpu.make_async_copy(fetched[i], target, fetch_sems.at[i])
            copy.start()
            fetches.append(copy)
        for copy in fetches:
            copy.wait()
    copies = []
    if last:
        field, sems = take(2)
        for i, earlier in enumerate(fields):
            copy = pltpu.make_async_copy(earlier, out.at[i], sems.at[i])
            copy.start()
            copies.append(copy)

    def table(name):
        at, shape = places[0][name]
        return narrow[at : at + shape[0], : shape[1]]

    def values(name, start, size):
        at, shape = places[1][name]
        return wide[at + start : at + start + size, :]

    if tick == 0:
        point_rows(sizes, values, slot, cell, amp, wave, aux)
    n_blocks = sy // SUB
    half = sx // 2
    at = sy + sx + 2 * TICKS
    w2 = aux[at : at + 1]
    eigen_x = [float(v) for v in basis(sx)[1].astype(np.float32)]

    zt = table("z")
    west_rows = along_z(west[...].reshape(2 * DEPTH * sy, sz), zt).reshape(2, DEPTH, sy, sz)
    for d in range(DEPTH):
        west_hat[d] = from_left(table("y"), jnp.concatenate([west_rows[0, d], west_rows[1, d]], axis=1))
    south_rows = along_z(south[...].reshape(2 * DEPTH * sx, sz), zt).reshape(2, DEPTH * sx, sz)
    n_south = DEPTH * sx
    south_hat[:n_south] = from_left(table("south"), jnp.concatenate([south_rows[0], south_rows[1]], axis=1))
    for c in range(2):
        row = sy + sx + 2 * tick + c
        south_hat[n_south:, c * sz : (c + 1) * sz] = aux[sy : sy + sx] * aux[row : row + 1]
    damping = jnp.broadcast_to(-DAMPING * w2, (SUB, sz))
    damping_square = damping * damping

    for j in range(n_blocks):
        here = slice(j * SUB, (j + 1) * SUB)
        high, low = split(west_hat[:, here, :].reshape(DEPTH * SUB, 2 * sz))
        west_table = table("west")
        n = DEPTH * SUB
        coeffs = dot(
            jnp.concatenate([west_table[:, :n], west_table[:, :n], west_table[:, n:]], axis=1),
            jnp.concatenate([high, low, high], axis=0),
        )
        base = values("eigen", j * SUB, SUB) - w2
        reach = [values("reach", d * sy + j * SUB, SUB) for d in range(DEPTH)] + [aux[here]]
        new_re = []
        new_im = []
        for i, k in enumerate(order(sx)):
            line = slice(i * SUB, (i + 1) * SUB)
            c_re = coeffs[line, :sz]
            c_im = coeffs[line, sz:]
            for d in range(DEPTH + 1):
                row = k * DEPTH + d if d < DEPTH else n_south + k
                row = slice(row, row + 1)
                c_re += reach[d] * south_hat[row, :sz]
                c_im += reach[d] * south_hat[row, sz:]
            shifted = base + eigen_x[k]
            size = shifted * shifted + damping_square
            inverse = pl.reciprocal(size, approx=True)
            inverse = inverse * (2.0 - size * inverse)
            p = shifted * inverse
            q = damping * inverse
            new_re.append(c_re * p + c_im * q)
            new_im.append(c_im * p - c_re * q)
        lines = along_z(jnp.concatenate(new_re + new_im, axis=0), zt)
        n = half * SUB
        e = from_left(table("even"), jnp.concatenate([lines[:n], lines[2 * n : 3 * n]], axis=1))
        o = from_left(table("odd"), jnp.concatenate([lines[n : 2 * n], lines[3 * n :]], axis=1))
        grid[:half, here, :] = (e + o).reshape(half, SUB, 2 * sz)
        difference = e - o
        for x in range(half):
            grid[sx - 1 - x, here, :] = difference[x * SUB : (x + 1) * SUB]

    if tick == 0:
        y_pos = lax.broadcasted_iota(jnp.int32, (sy, 1), 0).astype(F32)
        as_f = lambda i: layers[:, i : i + 1].astype(F32)
        sigma_y = ramp(as_f(2), y_pos) + ramp(as_f(3), sy - 1.0 - y_pos)
        labels = region[...].astype(F32).T
        count = vel.shape[0]
        contrast = vel[...] - w2
        vh, vl = split(contrast)
        vel_rows = jnp.concatenate([vh, vl], axis=0)
        label_lane = (lax.broadcasted_iota(jnp.int32, (sy, 2 * count), 1) % count).astype(F32)

    for x in range(sx):
        raw = from_left(table("y"), grid[x])
        raw_re = raw[:, :sz]
        raw_im = raw[:, sz:]
        if tick == 0:
            hot = (labels[:, x : x + 1] == label_lane).astype(BF16)
            c = dot(hot, vel_rows)
            x_pos = jnp.full((1, 1), float(x), F32)
            sigma_x = ramp(as_f(0), x_pos) + ramp(as_f(1), sx - 1.0 - x_pos)
            sigma = PEAK * (sigma_x + sigma_y)
            inverse = 1.0 / (BASE * BASE + sigma * sigma)
            g_re = 1.0 + c * (BASE * inverse)
            g_im = -c * (sigma * inverse)
            gain_re[x] = g_re
            gain_im[x] = g_im
        else:
            g_re = gain_re[x]
            g_im = gain_im[x]
        f_re = raw_re * g_re - raw_im * g_im
        f_im = raw_im * g_re + raw_re * g_im
        field[0, x] = f_re.astype(BF16)
        field[1, x] = f_im.astype(BF16)
        if not last:
            if x >= sx - DEPTH:
                east[0, x - (sx - DEPTH)] = f_re
                east[1, x - (sx - DEPTH)] = f_im
            north[0, DEPTH * x : DEPTH * (x + 1), :] = f_re[sy - DEPTH :]
            north[1, DEPTH * x : DEPTH * (x + 1), :] = f_im[sy - DEPTH :]
        elif x % GROUP == GROUP - 1:
            span = pl.ds(x - GROUP + 1, GROUP)
            copy = pltpu.make_async_copy(field.at[:, span], out.at[tick, :, span], sems.at[len(copies)])
            copy.start()
            copies.append(copy)
    for copy in copies:
        copy.wait()


def run_tick(tick, sizes, places, args):
    sx, sy, sz = sizes
    vm = pl.BlockSpec(memory_space=pltpu.VMEM)
    last = tick + 1 == TICKS
    whole = jax.ShapeDtypeStruct((2, sx, sy, sz), BF16)
    scratch = [
        pltpu.VMEM((DEPTH, sy, 2 * sz), F32),
        pltpu.VMEM((sx * (DEPTH + 1), 2 * sz), F32),
        pltpu.VMEM((sx, sy, 2 * sz), F32),
    ]
    in_specs = [vm] * len(args)
    if last:
        out_shape = [jax.ShapeDtypeStruct((TICKS, *whole.shape), BF16)]
        out_specs = [pl.BlockSpec(memory_space=pl.ANY)]
        scratch += [pltpu.VMEM(whole.shape, BF16), pltpu.SemaphoreType.DMA((TICKS - 1 + sx // GROUP,))]
    else:
        out_shape = [
            jax.ShapeDtypeStruct((2, DEPTH, sy, sz), F32),
            jax.ShapeDtypeStruct((2, sx * DEPTH, sz), F32),
            whole,
        ]
        if tick == 0:
            in_specs = [pl.BlockSpec(memory_space=pltpu.HBM)] * len(args)
            narrow, wide = args[:2]
            args = [pltpu.with_memory_space_constraint(a, pltpu.HBM) if a.size > 1 else a for a in args]
            out_shape += [jax.ShapeDtypeStruct(t.shape, t.dtype) for t in (narrow, wide)]
            out_shape += [jax.ShapeDtypeStruct((aux_rows(sizes), sz), F32)]
            out_shape += [jax.ShapeDtypeStruct((sx, sy, sz), F32)] * 2
            scratch += [pltpu.VMEM(a.shape, a.dtype) for a in args[2:]] + [pltpu.SemaphoreType.DMA((len(args),))]
        out_specs = [vm] * len(out_shape)
    return pl.pallas_call(
        functools.partial(tick_kernel, tick, sizes, places),
        out_shape=out_shape,
        in_specs=in_specs,
        out_specs=out_specs,
        scratch_shapes=scratch,
        compiler_params=pltpu.CompilerParams(vmem_limit_bytes=24 * 1024 * 1024),
        name=f"tick{tick}",
    )(*args)


def local(west_in, south_in, region, pml_layers, vel_table, src_slot, src_cell, src_amp, wave_sq):
    sx, sy = region.shape
    sz = vel_table.shape[1]
    sizes = (sx, sy, sz)
    (narrow, narrow_at), (wide, wide_at) = constants(sx, sy, sz)
    places = (narrow_at, wide_at)
    args = [jnp.asarray(narrow), jnp.asarray(wide), west_in, south_in.reshape(2, sx * DEPTH, sz), region, vel_table]
    args += [pml_layers.reshape(1, 4), src_slot, src_cell, src_amp, wave_sq.reshape(1, 1)]
    east, north, field, *kept = run_tick(0, sizes, places, args)
    fields = [field]
    for tick in range(1, TICKS):
        west = shift(east, "gx")
        south = shift(north, "gy")
        if tick + 1 < TICKS:
            east, north, field = run_tick(tick, sizes, places, [*kept, west, south])
            fields.append(field)
    (out,) = run_tick(TICKS - 1, sizes, places, [*kept, west, south, *fields])
    return out


def solution(mesh):
    in_specs = (
        P(None, "gx", "gy", None),
        P(None, "gx", "gy", None),
        P("gx", "gy"),
        P(None, "gx", "gy"),
        P(),
        P("gx", "gy"),
        P("gx", "gy"),
        P(),
        P(),
    )
    out_specs = P(None, None, "gx", "gy", None)
    return jax.shard_map(local, mesh=mesh, in_specs=in_specs, out_specs=out_specs, check_vma=False)
```

```python
import functools

import jax
import jax.numpy as jnp
import ml_dtypes
import numpy as np
from jax import lax
from jax.experimental import pallas as pl
from jax.experimental.pallas import tpu as pltpu
from jax.sharding import PartitionSpec as P

DEPTH = 4
TICKS = 3
SUB = 8
GROUP = 4
DAMPING = 0.25
PEAK = 4.0
BASE = 6.0
F32 = jnp.float32
BF16 = jnp.bfloat16


def shift(array, axis):
    peers = lax.axis_size(axis)
    return lax.ppermute(array, axis, [(i, i + 1) for i in range(peers - 1)])


def basis(n):
    k = np.arange(1, n + 1, dtype=np.float64)
    table = np.sqrt(2.0 / (n + 1)) * np.sin(np.pi * np.outer(k, k) / (n + 1))
    return table, 2.0 - 2.0 * np.cos(np.pi * k / (n + 1))


def halves(table):
    high = table.astype(ml_dtypes.bfloat16)
    low = (table - high.astype(np.float64)).astype(ml_dtypes.bfloat16)
    return high, low


def stacked(table):
    high, low = halves(table)
    return np.block([[high, high], [low, np.zeros_like(low)]])


def constants(sx, sy, sz):
    bx, ex = basis(sx)
    by, ey = basis(sy)
    bz, ez = basis(sz)
    zh, zl = halves(bz)
    half = sx // 2
    eye = np.eye(SUB)
    narrow = {
        "z": np.block([[zh, zl], [zh, zl]]),
        "even": stacked(np.kron(bx[:half, 0::2], eye)),
        "odd": stacked(np.kron(bx[:half, 1::2], eye)),
        "y": stacked(by),
        "south": stacked(np.kron(bx, np.eye(DEPTH))),
        "west": np.concatenate(halves(np.kron(bx[order(sx), :DEPTH], eye)), axis=1),
    }
    wide = {
        "eigen": ey[:, None] + ez[None, :],
        "bx": bx,
        "by": by,
        "bz": bz,
        "reach": np.repeat(by[:, :DEPTH].T.reshape(DEPTH * sy, 1), sz, axis=1),
    }
    east = halves(np.kron(bx[sx - DEPTH :, order(sx)], eye))
    north = []
    for j in range(sy // SUB):
        north += halves(np.kron(np.eye(sx)[:, order(sx)], by[sy - DEPTH :, j * SUB : (j + 1) * SUB]))
    traces = np.concatenate([*east, *north])
    return pack(narrow, ml_dtypes.bfloat16), pack(wide, np.float32), traces


def order(sx):
    return list(range(0, sx, 2)) + list(range(1, sx, 2))


def pack(tables, dtype):
    width = max(t.shape[1] for t in tables.values())
    rows, places, at = [], {}, 0
    for name, t in tables.items():
        places[name] = (at, t.shape)
        rows.append(np.pad(t.astype(np.float64), ((0, 0), (0, width - t.shape[1]))))
        at += t.shape[0]
    return np.concatenate(rows).astype(dtype), places


def split(values):
    high = values.astype(BF16)
    low = (values - high.astype(F32)).astype(BF16)
    return high, low


def dot(a, b):
    return jnp.dot(a, b, preferred_element_type=F32)


def along_z(rows, z_table):
    high, low = split(rows)
    both = dot(jnp.concatenate([high, low], axis=1), z_table)
    size_z = rows.shape[1]
    return both[:, :size_z] + both[:, size_z:]


def from_left(table, rows):
    high, low = split(rows)
    both = dot(table, jnp.concatenate([high, low], axis=0))
    n = both.shape[0] // 2
    return both[:n] + both[n:]


def ramp(layers, distance):
    portion = jnp.maximum(layers - distance, 0.0) / jnp.maximum(layers, 1.0)
    return portion * portion


def point_rows(sizes, values, slot, cell, amp, wave, aux):
    sx, sy, sz = sizes
    bits = [size.bit_length() - 1 for size in sizes]
    number = cell[...]
    cell_x = lax.shift_right_logical(number, bits[1] + bits[2])
    cell_y = lax.shift_right_logical(number, bits[2]) & (sy - 1)
    cell_z = number & (sz - 1)

    def column(name, size, where):
        lane = lax.broadcasted_iota(jnp.int32, (size, sz), 1)
        return jnp.sum(jnp.where(lane == where, values(name, 0, size), 0.0), axis=1, keepdims=True)

    aux[:sy] = jnp.broadcast_to(column("by", sy, cell_y), (sy, sz))
    row = lax.broadcasted_iota(jnp.int32, (sz, sz), 0)
    bz_row = jnp.sum(jnp.where(row == cell_z, values("bz", 0, sz), 0.0), axis=0, keepdims=True)
    aux[sy : sy + sx] = column("bx", sx, cell_x) * bz_row
    first = lax.axis_size("gx") + lax.axis_size("gy") - 2 - lax.axis_index("gx") - lax.axis_index("gy")
    lane = lax.broadcasted_iota(jnp.int32, amp.shape, 1)
    at = sy + sx
    for tick in range(TICKS):
        strength = jnp.sum(jnp.where(lane == first + tick, amp[...], 0.0), axis=1, keepdims=True)
        strength = jnp.where(slot[...] == first + tick, strength, 0.0)
        aux[at + 2 * tick : at + 2 * tick + 2] = jnp.broadcast_to(strength, (2, sz))
    at += 2 * TICKS
    aux[at : at + 1] = jnp.broadcast_to(wave[...], (1, sz))


def aux_rows(sizes):
    sx, sy, _ = sizes
    return -(-(sx + sy + 2 * TICKS + 1) // SUB) * SUB


def table_of(narrow, places):
    def table(name):
        at, shape = places[name]
        return narrow[at : at + shape[0], : shape[1]]

    return table


def values_of(wide, places):
    def values(name, start, size):
        at, shape = places[name]
        return wide[at + start : at + start + size, :]

    return values


def wave_row(sizes, aux):
    at = sizes[0] + sizes[1] + 2 * TICKS
    return aux[at : at + 1]


def spread_west(sizes, table, west, west_hat):
    sx, sy, sz = sizes
    rows = along_z(west[...].reshape(2 * DEPTH * sy, sz), table("z")).reshape(2, DEPTH, sy, sz)
    for d in range(DEPTH):
        west_hat[d] = from_left(table("y"), jnp.concatenate([rows[0, d], rows[1, d]], axis=1))
    n = DEPTH * SUB
    west_table = table("west")
    left = jnp.concatenate([west_table[:, :n], west_table[:, :n], west_table[:, n:]], axis=1)
    blocks = []
    for j in range(sy // SUB):
        high, low = split(west_hat[:, j * SUB : (j + 1) * SUB, :].reshape(n, 2 * sz))
        blocks.append(dot(left, jnp.concatenate([high, low, high], axis=0)))
    return blocks


def transform_south(sizes, table, south, south_hat):
    sx, _, sz = sizes
    n = DEPTH * sx
    rows = along_z(south[...].reshape(2 * n, sz), table("z")).reshape(2, n, sz)
    south_hat[:n] = from_left(table("south"), jnp.concatenate([rows[0], rows[1]], axis=1))


def place_point(tick, sizes, aux, south_hat):
    sx, sy, sz = sizes
    for c in range(2):
        row = sy + sx + 2 * tick + c
        south_hat[DEPTH * sx :, c * sz : (c + 1) * sz] = aux[sy : sy + sx] * aux[row : row + 1]


def spectrum_block(j, sizes, coeffs, values, aux, south_hat):
    sx, sy, sz = sizes
    here = slice(j * SUB, (j + 1) * SUB)
    eigen_x = [float(v) for v in basis(sx)[1].astype(np.float32)]
    w2 = wave_row(sizes, aux)
    damping = jnp.broadcast_to(-DAMPING * w2, (SUB, sz))
    damping_square = damping * damping
    base = values("eigen", j * SUB, SUB) - w2
    reach = [values("reach", d * sy + j * SUB, SUB) for d in range(DEPTH)] + [aux[here]]
    new_re = []
    new_im = []
    for i, k in enumerate(order(sx)):
        line = slice(i * SUB, (i + 1) * SUB)
        c_re = coeffs[line, :sz]
        c_im = coeffs[line, sz:]
        for d in range(DEPTH + 1):
            row = k * DEPTH + d if d < DEPTH else sx * DEPTH + k
            row = slice(row, row + 1)
            c_re += reach[d] * south_hat[row, :sz]
            c_im += reach[d] * south_hat[row, sz:]
        shifted = base + eigen_x[k]
        size = shifted * shifted + damping_square
        inverse = pl.reciprocal(size, approx=True)
        inverse = inverse * (2.0 - size * inverse)
        p = shifted * inverse
        q = damping * inverse
        new_re.append(c_re * p + c_im * q)
        new_im.append(c_im * p - c_re * q)
    return jnp.concatenate(new_re, axis=0), jnp.concatenate(new_im, axis=0)


def invert_block(j, sizes, table, rows, grid):
    sx, _, sz = sizes
    half = sx // 2
    here = slice(j * SUB, (j + 1) * SUB)
    lines = along_z(rows, table("z"))
    n = half * SUB
    e = from_left(table("even"), jnp.concatenate([lines[:n], lines[2 * n : 3 * n]], axis=1))
    o = from_left(table("odd"), jnp.concatenate([lines[n : 2 * n], lines[3 * n :]], axis=1))
    grid[:half, here, :] = (e + o).reshape(half, SUB, 2 * sz)
    difference = e - o
    for x in range(half):
        grid[sx - 1 - x, here, :] = difference[x * SUB : (x + 1) * SUB]


def gains_of(sizes, layers, vel, w2):
    sx, sy, _ = sizes
    count = vel.shape[0]
    layer = [layers[:, i : i + 1].astype(F32) for i in range(4)]
    rows = jnp.concatenate(split(vel[...] - w2), axis=0)

    def gains(labels, x_pos, y_pos):
        n = labels.shape[0]
        lane = (lax.broadcasted_iota(jnp.int32, (n, 2 * count), 1) % count).astype(F32)
        contrast = dot((labels == lane).astype(BF16), rows)
        sigma = ramp(layer[0], x_pos) + ramp(layer[1], sx - 1.0 - x_pos)
        sigma = PEAK * (sigma + ramp(layer[2], y_pos) + ramp(layer[3], sy - 1.0 - y_pos))
        inverse = 1.0 / (BASE * BASE + sigma * sigma)
        return 1.0 + contrast * (BASE * inverse), -contrast * (sigma * inverse)

    return gains


def y_places(sizes):
    return lax.broadcasted_iota(jnp.int32, (sizes[1], 1), 0).astype(F32)


def correct(raw_re, raw_im, g_re, g_im):
    return raw_re * g_re - raw_im * g_im, raw_im * g_re + raw_re * g_im


def trace_gains(sizes, region, vel, layers, wave, gain_east, gain_north):
    sx, sy, _ = sizes
    n_north = DEPTH * sx
    gains = gains_of(sizes, layers, vel, wave[...])
    labels = region[...].astype(F32)
    columns = labels.T
    for d in range(DEPTH):
        x = sx - DEPTH + d
        g_re, g_im = gains(columns[:, x : x + 1], jnp.full((1, 1), float(x), F32), y_places(sizes))
        gain_east[0, d] = g_re
        gain_east[1, d] = g_im
    row = lax.broadcasted_iota(jnp.int32, (n_north, sx), 0)
    repeat = (row // DEPTH == lax.broadcasted_iota(jnp.int32, (n_north, sx), 1)).astype(BF16)
    spread = dot(repeat, labels.astype(BF16))
    row = lax.broadcasted_iota(jnp.int32, (n_north, sy), 0)
    lane = lax.broadcasted_iota(jnp.int32, (n_north, sy), 1)
    mine = jnp.sum(jnp.where(lane == sy - DEPTH + row % DEPTH, spread, 0.0), axis=1, keepdims=True)
    row = lax.broadcasted_iota(jnp.int32, (n_north, 1), 0)
    x_pos = (row // DEPTH).astype(F32)
    y_pos = (sy - DEPTH + row % DEPTH).astype(F32)
    g_re, g_im = gains(mine, x_pos, y_pos)
    gain_north[0] = g_re
    gain_north[1] = g_im


def traces_kernel(tick, sizes, places, *refs):
    sx, sy, sz = sizes
    refs = list(refs)
    take = lambda n: [refs.pop(0) for _ in range(n)]
    waits = []
    if tick == 0:
        fetched = take(12)
        fetched = fetched[4:8] + fetched[9:] + fetched[:4] + fetched[8:9]
        east, north, spectrum, narrow, wide, tall, aux, gain_east, gain_north, region, vel, layers = take(12)
    else:
        narrow, wide, tall, aux, gain_east, gain_north, from_west, south = take(8)
        east, north, spectrum = take(3)
    south_hat, east_hat = take(2)
    if tick == 0:
        west_hat, west, south, slot, cell, amp, wave = take(7)
        (fetch_sems,) = take(1)
        targets = [slot, cell, amp, wave, region, vel, layers, narrow, west, south, wide, tall]
        for i, target in enumerate(targets):
            copy = pltpu.make_async_copy(fetched[i], target, fetch_sems.at[i])
            copy.start()
            waits.append(copy)
        for copy in waits[:7]:
            copy.wait()
    table = table_of(narrow, places[0])
    values = values_of(wide, places[1])
    n_east = DEPTH * SUB
    n_north = DEPTH * sx
    if tick == 0:
        trace_gains(sizes, region, vel, layers, wave, gain_east, gain_north)
        for copy in waits[7:10]:
            copy.wait()
        starts = spread_west(sizes, table, west, west_hat)
    transform_south(sizes, table, south, south_hat)
    if tick == 0:
        for copy in waits[10:]:
            copy.wait()
        point_rows(sizes, values, slot, cell, amp, wave, aux)
    else:
        starts = [from_west[j] for j in range(sy // SUB)]
    place_point(tick, sizes, aux, south_hat)
    total = jnp.zeros((n_north, 2 * sz), F32)
    blocks = [spectrum_block(j, sizes, starts[j], values, aux, south_hat) for j in range(sy // SUB)]
    for j in range(sy // SUB):
        here = slice(j * SUB, (j + 1) * SUB)
        re, im = blocks[j]
        n = re.shape[0]
        spectrum[j, :n] = re
        spectrum[j, n:] = im
        high, low = split(jnp.concatenate([re, im], axis=1))
        east_table = tall[: 2 * n_east]
        start = 2 * n_east + 2 * n_north * j
        north_table = tall[start : start + 2 * n_north]
        main = dot(jnp.concatenate([east_table, north_table], axis=0), high)
        rest = dot(jnp.concatenate([east_table[:n_east], north_table[:n_north]], axis=0), low)
        part = main[:n_east] + main[n_east : 2 * n_east] + rest[:n_east]
        east_hat[:, here, :] = part.reshape(DEPTH, SUB, 2 * sz)
        at = 2 * n_east
        total += main[at : at + n_north] + main[at + n_north :] + rest[n_east:]

    zt = table("z")
    planes = [from_left(table("y"), east_hat[d]) for d in range(DEPTH)]
    lines = [p[:, :sz] for p in planes] + [p[:, sz:] for p in planes]
    lines = along_z(jnp.concatenate(lines, axis=0), zt).reshape(2, DEPTH, sy, sz)
    east[0], east[1] = correct(lines[0], lines[1], gain_east[0], gain_east[1])
    rows = from_left(table("south"), total)
    lines = along_z(jnp.concatenate([rows[:, :sz], rows[:, sz:]], axis=0), zt)
    north[0], north[1] = correct(lines[:n_north], lines[n_north:], gain_north[0], gain_north[1])


def west_kernel(sizes, places, narrow, west, _, out, west_hat):
    for j, block in enumerate(spread_west(sizes, table_of(narrow, places[0]), west, west_hat)):
        out[j] = block


def field_kernel(tick, sizes, places, *refs):
    sx, sy, sz = sizes
    refs = list(refs)
    take = lambda n: [refs.pop(0) for _ in range(n)]
    if tick == 0:
        narrow, spectrum, aux, region, vel, layers = take(6)
        field, gain_re, gain_im = take(3)
    else:
        narrow, spectrum, gain_re, gain_im = take(4)
        (field,) = take(1)
    (grid,) = take(1)
    table = table_of(narrow, places[0])
    for j in range(sy // SUB):
        invert_block(j, sizes, table, spectrum[j], grid)
    if tick == 0:
        gains = gains_of(sizes, layers, vel, wave_row(sizes, aux))
        columns = region[...].astype(F32).T
    for x in range(sx):
        raw = from_left(table("y"), grid[x])
        if tick == 0:
            g_re, g_im = gains(columns[:, x : x + 1], jnp.full((1, 1), float(x), F32), y_places(sizes))
            gain_re[x] = g_re
            gain_im[x] = g_im
        else:
            g_re, g_im = gain_re[x], gain_im[x]
        f_re, f_im = correct(raw[:, :sz], raw[:, sz:], g_re, g_im)
        field[0, x] = f_re.astype(BF16)
        field[1, x] = f_im.astype(BF16)


def last_kernel(tick, sizes, places, *refs):
    sx, sy, sz = sizes
    narrow, wide, aux, gain_re, gain_im, from_west, south = refs[:7]
    fields = refs[7 : 7 + tick]
    out, south_hat, grid, field, sems = refs[7 + tick :]
    copies = []
    for i, earlier in enumerate(fields):
        copy = pltpu.make_async_copy(earlier, out.at[i], sems.at[i])
        copy.start()
        copies.append(copy)
    table = table_of(narrow, places[0])
    values = values_of(wide, places[1])
    transform_south(sizes, table, south, south_hat)
    place_point(tick, sizes, aux, south_hat)
    blocks = [
        jnp.concatenate(spectrum_block(j, sizes, from_west[j], values, aux, south_hat), axis=0)
        for j in range(sy // SUB)
    ]
    for j in range(sy // SUB):
        invert_block(j, sizes, table, blocks[j], grid)
    for x in range(sx):
        raw = from_left(table("y"), grid[x])
        f_re, f_im = correct(raw[:, :sz], raw[:, sz:], gain_re[x], gain_im[x])
        field[0, x] = f_re.astype(BF16)
        field[1, x] = f_im.astype(BF16)
        if x % GROUP == GROUP - 1:
            span = pl.ds(x - GROUP + 1, GROUP)
            copy = pltpu.make_async_copy(field.at[:, span], out.at[tick, :, span], sems.at[len(copies)])
            copy.start()
            copies.append(copy)
    for copy in copies:
        copy.wait()


def call(kernel, name, args, out_shape, scratch, cost, in_specs=None, out_specs=None):
    vm = pl.BlockSpec(memory_space=pltpu.VMEM)
    return pl.pallas_call(
        kernel,
        out_shape=out_shape,
        in_specs=in_specs or [vm] * len(args),
        out_specs=out_specs or [vm] * len(out_shape),
        scratch_shapes=scratch,
        cost_estimate=pl.CostEstimate(flops=cost, bytes_accessed=4 << 20, transcendentals=0),
        compiler_params=pltpu.CompilerParams(vmem_limit_bytes=24 * 1024 * 1024),
        name=name,
    )(*args)


def local(west_in, south_in, region, pml_layers, vel_table, src_slot, src_cell, src_amp, wave_sq):
    sx, sy = region.shape
    sz = vel_table.shape[1]
    sizes = (sx, sy, sz)
    (narrow, narrow_at), (wide, wide_at), tall = constants(sx, sy, sz)
    places = (narrow_at, wide_at)
    shape = jax.ShapeDtypeStruct
    like = lambda a: shape(a.shape, a.dtype)
    vm = pl.BlockSpec(memory_space=pltpu.VMEM)
    west_hat = pltpu.VMEM((DEPTH, sy, 2 * sz), F32)
    south_hat = pltpu.VMEM((sx * (DEPTH + 1), 2 * sz), F32)
    hats = [south_hat, west_hat]
    west_shape = shape((sy // SUB, sx * SUB, 2 * sz), F32)
    grid = pltpu.VMEM((sx, sy, 2 * sz), F32)
    trace_shapes = [shape((2, DEPTH, sy, sz), F32), shape((2, sx * DEPTH, sz), F32)]
    spectrum_shape = shape((sy // SUB, 2 * sx * SUB, sz), F32)
    field_shape = shape((2, sx, sy, sz), BF16)
    gain_shapes = [shape((sx, sy, sz), F32)] * 2
    cost = 10**9

    south = south_in.reshape(2, sx * DEPTH, sz)
    tables = [jnp.asarray(t) for t in (narrow, wide, tall)]
    layers = pml_layers.reshape(1, 4)
    args = [tables[0], west_in, south, tables[1], src_slot, src_cell, src_amp, wave_sq.reshape(1, 1), tables[2]]
    args += [region, vel_table, layers]
    args = [pltpu.with_memory_space_constraint(a, pltpu.HBM) if a.size > 1 else a for a in args]
    moved = [west_in, south, src_slot, src_cell, src_amp, wave_sq.reshape(1, 1)]
    res = call(
        functools.partial(traces_kernel, 0, sizes, places),
        "traces0",
        args,
        trace_shapes
        + [spectrum_shape]
        + [like(t) for t in tables]
        + [shape((aux_rows(sizes), sz), F32)]
        + trace_shapes
        + [like(region), like(vel_table), like(layers)],
        hats + [west_hat] + [pltpu.VMEM(m.shape, m.dtype) for m in moved] + [pltpu.SemaphoreType.DMA((len(args),))],
        cost,
        in_specs=[pl.BlockSpec(memory_space=pltpu.HBM)] * len(args),
    )
    east, north, spectrum, narrow, wide, tall, aux, gain_east, gain_north, region, vel_table, layers = res
    fields = []
    gains = None
    for tick in range(1, TICKS):
        west = shift(east, "gx")
        south = shift(north, "gy")
        if tick == 1:
            given = [narrow, spectrum, aux, region, vel_table, layers]
            results = [field_shape, *gain_shapes]
        else:
            given = [narrow, spectrum, *gains]
            results = [field_shape]
        field, *made = call(
            functools.partial(field_kernel, tick - 1, sizes, places), f"field{tick - 1}", given, results, [grid], cost
        )
        gains = made or gains
        fields.append(field)
        (from_west,) = call(
            functools.partial(west_kernel, sizes, places),
            f"west{tick}",
            [narrow, west, field],
            [west_shape],
            [west_hat],
            cost,
            in_specs=[vm, vm, pl.BlockSpec(memory_space=pl.ANY)],
        )
        if tick + 1 < TICKS:
            east, north, spectrum = call(
                functools.partial(traces_kernel, tick, sizes, places),
                f"traces{tick}",
                [narrow, wide, tall, aux, gain_east, gain_north, from_west, south],
                trace_shapes + [spectrum_shape],
                hats,
                cost,
            )
    given = [narrow, wide, aux, *gains, from_west, south, *fields]
    (out,) = call(
        functools.partial(last_kernel, TICKS - 1, sizes, places),
        "last",
        given,
        [shape((TICKS, *field_shape.shape), BF16)],
        [south_hat, grid, pltpu.VMEM(field_shape.shape, BF16), pltpu.SemaphoreType.DMA((TICKS - 1 + sx // GROUP,))],
        cost,
        out_specs=[pl.BlockSpec(memory_space=pl.ANY)],
    )
    return out


def solution(mesh):
    in_specs = (
        P(None, "gx", "gy", None),
        P(None, "gx", "gy", None),
        P("gx", "gy"),
        P(None, "gx", "gy"),
        P(),
        P("gx", "gy"),
        P("gx", "gy"),
        P(),
        P(),
    )
    out_specs = P(None, None, "gx", "gy", None)
    return jax.shard_map(local, mesh=mesh, in_specs=in_specs, out_specs=out_specs, check_vma=False)
```

```python
import functools

import jax
import jax.numpy as jnp
import ml_dtypes
import numpy as np
from jax import lax
from jax.experimental import pallas as pl
from jax.experimental.pallas import tpu as pltpu
from jax.sharding import PartitionSpec as P

DEPTH = 4
TICKS = 3
SUB = 8
GROUP = 4
DAMPING = 0.25
PEAK = 4.0
BASE = 6.0
F32 = jnp.float32
BF16 = jnp.bfloat16


def shift(array, axis):
    peers = lax.axis_size(axis)
    return lax.ppermute(array, axis, [(i, i + 1) for i in range(peers - 1)])


def basis(n):
    k = np.arange(1, n + 1, dtype=np.float64)
    table = np.sqrt(2.0 / (n + 1)) * np.sin(np.pi * np.outer(k, k) / (n + 1))
    return table, 2.0 - 2.0 * np.cos(np.pi * k / (n + 1))


def halves(table):
    high = table.astype(ml_dtypes.bfloat16)
    low = (table - high.astype(np.float64)).astype(ml_dtypes.bfloat16)
    return high, low


def stacked(table):
    high, low = halves(table)
    return np.block([[high, high], [low, np.zeros_like(low)]])


def constants(sx, sy, sz):
    bx, ex = basis(sx)
    by, ey = basis(sy)
    bz, ez = basis(sz)
    zh, zl = halves(bz)
    half = sx // 2
    eye = np.eye(SUB)
    narrow = {
        "z": np.block([[zh, zl], [zh, zl]]),
        "even": stacked(np.kron(bx[:half, 0::2], eye)),
        "odd": stacked(np.kron(bx[:half, 1::2], eye)),
        "y": stacked(by),
        "south": stacked(np.kron(bx, np.eye(DEPTH))),
        "west": np.concatenate(halves(np.kron(bx[order(sx), :DEPTH], eye)), axis=1),
    }
    wide = {
        "eigen": ey[:, None] + ez[None, :],
        "bx": bx,
        "by": by,
        "bz": bz,
        "reach": np.repeat(by[:, :DEPTH].T.reshape(DEPTH * sy, 1), sz, axis=1),
    }
    east = halves(np.kron(bx[sx - DEPTH :, order(sx)], eye))
    north = []
    for j in range(sy // SUB):
        north += halves(np.kron(np.eye(sx)[:, order(sx)], by[sy - DEPTH :, j * SUB : (j + 1) * SUB]))
    traces = np.concatenate([*east, *north])
    return pack(narrow, ml_dtypes.bfloat16), pack(wide, np.float32), traces


def order(sx):
    return list(range(0, sx, 2)) + list(range(1, sx, 2))


def pack(tables, dtype):
    width = max(t.shape[1] for t in tables.values())
    rows, places, at = [], {}, 0
    for name, t in tables.items():
        places[name] = (at, t.shape)
        rows.append(np.pad(t.astype(np.float64), ((0, 0), (0, width - t.shape[1]))))
        at += t.shape[0]
    return np.concatenate(rows).astype(dtype), places


def split(values):
    high = values.astype(BF16)
    low = (values - high.astype(F32)).astype(BF16)
    return high, low


def dot(a, b):
    return jnp.dot(a, b, preferred_element_type=F32)


def along_z(rows, z_table):
    high, low = split(rows)
    both = dot(jnp.concatenate([high, low], axis=1), z_table)
    size_z = rows.shape[1]
    return both[:, :size_z] + both[:, size_z:]


def from_left(table, rows):
    high, low = split(rows)
    both = dot(table, jnp.concatenate([high, low], axis=0))
    n = both.shape[0] // 2
    return both[:n] + both[n:]


def ramp(layers, distance):
    portion = jnp.maximum(layers - distance, 0.0) / jnp.maximum(layers, 1.0)
    return portion * portion


def point_rows(sizes, values, slot, cell, amp, wave, aux):
    sx, sy, sz = sizes
    bits = [size.bit_length() - 1 for size in sizes]
    number = cell[...]
    cell_x = lax.shift_right_logical(number, bits[1] + bits[2])
    cell_y = lax.shift_right_logical(number, bits[2]) & (sy - 1)
    cell_z = number & (sz - 1)

    def column(name, size, where):
        lane = lax.broadcasted_iota(jnp.int32, (size, sz), 1)
        return jnp.sum(jnp.where(lane == where, values(name, 0, size), 0.0), axis=1, keepdims=True)

    aux[:sy] = jnp.broadcast_to(column("by", sy, cell_y), (sy, sz))
    row = lax.broadcasted_iota(jnp.int32, (sz, sz), 0)
    bz_row = jnp.sum(jnp.where(row == cell_z, values("bz", 0, sz), 0.0), axis=0, keepdims=True)
    aux[sy : sy + sx] = column("bx", sx, cell_x) * bz_row
    first = lax.axis_size("gx") + lax.axis_size("gy") - 2 - lax.axis_index("gx") - lax.axis_index("gy")
    lane = lax.broadcasted_iota(jnp.int32, amp.shape, 1)
    at = sy + sx
    for tick in range(TICKS):
        strength = jnp.sum(jnp.where(lane == first + tick, amp[...], 0.0), axis=1, keepdims=True)
        strength = jnp.where(slot[...] == first + tick, strength, 0.0)
        aux[at + 2 * tick : at + 2 * tick + 2] = jnp.broadcast_to(strength, (2, sz))
    at += 2 * TICKS
    aux[at : at + 1] = jnp.broadcast_to(wave[...], (1, sz))


def aux_rows(sizes):
    sx, sy, _ = sizes
    return -(-(sx + sy + 2 * TICKS + 1) // SUB) * SUB


def table_of(narrow, places):
    def table(name):
        at, shape = places[name]
        return narrow[at : at + shape[0], : shape[1]]

    return table


def values_of(wide, places):
    def values(name, start, size):
        at, shape = places[name]
        return wide[at + start : at + start + size, :]

    return values


def wave_row(sizes, aux):
    at = sizes[0] + sizes[1] + 2 * TICKS
    return aux[at : at + 1]


def spread_west(sizes, table, west, west_hat):
    sx, sy, sz = sizes
    rows = along_z(west[...].reshape(2 * DEPTH * sy, sz), table("z")).reshape(2, DEPTH, sy, sz)
    for d in range(DEPTH):
        west_hat[d] = from_left(table("y"), jnp.concatenate([rows[0, d], rows[1, d]], axis=1))
    n = DEPTH * SUB
    west_table = table("west")
    left = jnp.concatenate([west_table[:, :n], west_table[:, :n], west_table[:, n:]], axis=1)
    blocks = []
    for j in range(sy // SUB):
        high, low = split(west_hat[:, j * SUB : (j + 1) * SUB, :].reshape(n, 2 * sz))
        blocks.append(dot(left, jnp.concatenate([high, low, high], axis=0)))
    return blocks


def transform_south(sizes, table, south, south_hat):
    sx, _, sz = sizes
    n = DEPTH * sx
    rows = along_z(south[...].reshape(2 * n, sz), table("z")).reshape(2, n, sz)
    south_hat[:n] = from_left(table("south"), jnp.concatenate([rows[0], rows[1]], axis=1))


def place_point(tick, sizes, aux, point_hat):
    sx, sy, sz = sizes
    for c in range(2):
        row = sy + sx + 2 * tick + c
        point_hat[:, c * sz : (c + 1) * sz] = aux[sy : sy + sx] * aux[row : row + 1]


def inverse_symbol(j, sizes, values, aux):
    sx, _, sz = sizes
    eigen_x = [float(v) for v in basis(sx)[1].astype(np.float32)]
    w2 = wave_row(sizes, aux)
    damping = jnp.broadcast_to(-DAMPING * w2, (SUB, sz))
    damping_square = damping * damping
    base = values("eigen", j * SUB, SUB) - w2
    pairs = []
    for k in order(sx):
        shifted = base + eigen_x[k]
        size = shifted * shifted + damping_square
        inverse = pl.reciprocal(size, approx=True)
        inverse = inverse * (2.0 - size * inverse)
        pairs.append((shifted * inverse, damping * inverse))
    return pairs


def spectrum_block(j, sizes, coeffs, values, pairs, south_hat, point=None):
    sx, sy, sz = sizes
    reach = [values("reach", d * sy + j * SUB, SUB) for d in range(DEPTH)]
    if point is not None:
        reach.append(point)
    new_re = []
    new_im = []
    for i, k in enumerate(order(sx)):
        line = slice(i * SUB, (i + 1) * SUB)
        c_re = coeffs[line, :sz]
        c_im = coeffs[line, sz:]
        for d, factor in enumerate(reach):
            row = k * DEPTH + d if d < DEPTH else sx * DEPTH + k
            row = slice(row, row + 1)
            c_re += factor * south_hat[row, :sz]
            c_im += factor * south_hat[row, sz:]
        p, q = pairs[i]
        new_re.append(c_re * p + c_im * q)
        new_im.append(c_im * p - c_re * q)
    return jnp.concatenate(new_re, axis=0), jnp.concatenate(new_im, axis=0)


def kept_pairs(j, sizes, symbol):
    return [tuple(symbol[c, j, i * SUB : (i + 1) * SUB] for c in range(2)) for i in range(sizes[0])]


def invert_block(j, sizes, table, rows, grid):
    sx, _, sz = sizes
    half = sx // 2
    here = slice(j * SUB, (j + 1) * SUB)
    lines = along_z(rows, table("z"))
    n = half * SUB
    e = from_left(table("even"), jnp.concatenate([lines[:n], lines[2 * n : 3 * n]], axis=1))
    o = from_left(table("odd"), jnp.concatenate([lines[n : 2 * n], lines[3 * n :]], axis=1))
    grid[:half, here, :] = (e + o).reshape(half, SUB, 2 * sz)
    difference = e - o
    for x in range(half):
        grid[sx - 1 - x, here, :] = difference[x * SUB : (x + 1) * SUB]


def gains_of(sizes, layers, vel, w2):
    sx, sy, _ = sizes
    count = vel.shape[0]
    layer = [layers[:, i : i + 1].astype(F32) for i in range(4)]
    rows = jnp.concatenate(split(vel[...] - w2), axis=0)

    def gains(labels, x_pos, y_pos):
        n = labels.shape[0]
        lane = (lax.broadcasted_iota(jnp.int32, (n, 2 * count), 1) % count).astype(F32)
        contrast = dot((labels == lane).astype(BF16), rows)
        sigma = ramp(layer[0], x_pos) + ramp(layer[1], sx - 1.0 - x_pos)
        sigma = PEAK * (sigma + ramp(layer[2], y_pos) + ramp(layer[3], sy - 1.0 - y_pos))
        inverse = 1.0 / (BASE * BASE + sigma * sigma)
        return 1.0 + contrast * (BASE * inverse), -contrast * (sigma * inverse)

    return gains


def y_places(sizes):
    return lax.broadcasted_iota(jnp.int32, (sizes[1], 1), 0).astype(F32)


def correct(raw_re, raw_im, g_re, g_im):
    return raw_re * g_re - raw_im * g_im, raw_im * g_re + raw_re * g_im


def trace_gains(sizes, region, vel, layers, wave, gain_east, gain_north):
    sx, sy, _ = sizes
    n_north = DEPTH * sx
    gains = gains_of(sizes, layers, vel, wave[...])
    labels = region[...].astype(F32)
    columns = labels.T
    for d in range(DEPTH):
        x = sx - DEPTH + d
        g_re, g_im = gains(columns[:, x : x + 1], jnp.full((1, 1), float(x), F32), y_places(sizes))
        gain_east[0, d] = g_re
        gain_east[1, d] = g_im
    row = lax.broadcasted_iota(jnp.int32, (n_north, sx), 0)
    repeat = (row // DEPTH == lax.broadcasted_iota(jnp.int32, (n_north, sx), 1)).astype(BF16)
    spread = dot(repeat, labels.astype(BF16))
    row = lax.broadcasted_iota(jnp.int32, (n_north, sy), 0)
    lane = lax.broadcasted_iota(jnp.int32, (n_north, sy), 1)
    mine = jnp.sum(jnp.where(lane == sy - DEPTH + row % DEPTH, spread, 0.0), axis=1, keepdims=True)
    row = lax.broadcasted_iota(jnp.int32, (n_north, 1), 0)
    x_pos = (row // DEPTH).astype(F32)
    y_pos = (sy - DEPTH + row % DEPTH).astype(F32)
    g_re, g_im = gains(mine, x_pos, y_pos)
    gain_north[0] = g_re
    gain_north[1] = g_im


def traces_kernel(tick, sizes, places, *refs):
    sx, sy, sz = sizes
    refs = list(refs)
    take = lambda n: [refs.pop(0) for _ in range(n)]
    waits = []
    if tick == 0:
        fetched = take(12)
        fetched = fetched[4:8] + fetched[9:] + fetched[:4] + fetched[8:9]
        east, north, spectrum, narrow, wide, tall, aux, gain_east, gain_north, region, vel, layers = take(12)
    else:
        narrow, wide, tall, symbol, gain_east, gain_north, from_west, south = take(8)
        east, north, spectrum = take(3)
    south_hat, east_hat = take(2)
    if tick == 0:
        west_hat, west, south, slot, cell, amp, wave = take(7)
        (fetch_sems,) = take(1)
        targets = [slot, cell, amp, wave, region, vel, layers, narrow, west, south, wide, tall]
        for i, target in enumerate(targets):
            copy = pltpu.make_async_copy(fetched[i], target, fetch_sems.at[i])
            copy.start()
            waits.append(copy)
        for copy in waits[:7]:
            copy.wait()
    table = table_of(narrow, places[0])
    values = values_of(wide, places[1])
    n_east = DEPTH * SUB
    n_north = DEPTH * sx
    if tick == 0:
        trace_gains(sizes, region, vel, layers, wave, gain_east, gain_north)
        for copy in waits[7:10]:
            copy.wait()
        starts = spread_west(sizes, table, west, west_hat)
    transform_south(sizes, table, south, south_hat)
    if tick == 0:
        for copy in waits[10:]:
            copy.wait()
        point_rows(sizes, values, slot, cell, amp, wave, aux)
        place_point(tick, sizes, aux, south_hat.at[DEPTH * sx :])
    else:
        starts = [from_west[j] for j in range(sy // SUB)]
    total = jnp.zeros((n_north, 2 * sz), F32)
    blocks = []
    for j in range(sy // SUB):
        pairs = inverse_symbol(j, sizes, values, aux) if tick == 0 else kept_pairs(j, sizes, symbol)
        point = aux[j * SUB : (j + 1) * SUB] if tick == 0 else None
        blocks.append(spectrum_block(j, sizes, starts[j], values, pairs, south_hat, point))
    for j in range(sy // SUB):
        here = slice(j * SUB, (j + 1) * SUB)
        re, im = blocks[j]
        n = re.shape[0]
        spectrum[j, :n] = re
        spectrum[j, n:] = im
        high, low = split(jnp.concatenate([re, im], axis=1))
        east_table = tall[: 2 * n_east]
        start = 2 * n_east + 2 * n_north * j
        north_table = tall[start : start + 2 * n_north]
        main = dot(jnp.concatenate([east_table, north_table], axis=0), high)
        rest = dot(jnp.concatenate([east_table[:n_east], north_table[:n_north]], axis=0), low)
        part = main[:n_east] + main[n_east : 2 * n_east] + rest[:n_east]
        east_hat[:, here, :] = part.reshape(DEPTH, SUB, 2 * sz)
        at = 2 * n_east
        total += main[at : at + n_north] + main[at + n_north :] + rest[n_east:]

    zt = table("z")
    planes = [from_left(table("y"), east_hat[d]) for d in range(DEPTH)]
    lines = [p[:, :sz] for p in planes] + [p[:, sz:] for p in planes]
    lines = along_z(jnp.concatenate(lines, axis=0), zt).reshape(2, DEPTH, sy, sz)
    east[0], east[1] = correct(lines[0], lines[1], gain_east[0], gain_east[1])
    rows = from_left(table("south"), total)
    lines = along_z(jnp.concatenate([rows[:, :sz], rows[:, sz:]], axis=0), zt)
    north[0], north[1] = correct(lines[:n_north], lines[n_north:], gain_north[0], gain_north[1])


def west_kernel(tick, sizes, places, narrow, aux, west, _, out, west_hat, point_hat):
    sx, _, sz = sizes
    place_point(tick, sizes, aux, point_hat)
    for j, block in enumerate(spread_west(sizes, table_of(narrow, places[0]), west, west_hat)):
        factor = aux[j * SUB : (j + 1) * SUB]
        for i, k in enumerate(order(sx)):
            line = slice(i * SUB, (i + 1) * SUB)
            for part in (slice(0, sz), slice(sz, 2 * sz)):
                out[j, line, part] = block[line, part] + factor * point_hat[k : k + 1, part]


def field_kernel(tick, sizes, places, *refs):
    sx, sy, sz = sizes
    refs = list(refs)
    take = lambda n: [refs.pop(0) for _ in range(n)]
    if tick == 0:
        narrow, spectrum, aux, region, vel, layers, wide = take(7)
        field, gain_re, gain_im, symbol = take(4)
        values = values_of(wide, places[1])
        for j in range(sy // SUB):
            for i, pair in enumerate(inverse_symbol(j, sizes, values, aux)):
                for c in range(2):
                    symbol[c, j, i * SUB : (i + 1) * SUB] = pair[c]
    else:
        narrow, spectrum, gain_re, gain_im = take(4)
        (field,) = take(1)
    (grid,) = take(1)
    table = table_of(narrow, places[0])
    for j in range(sy // SUB):
        invert_block(j, sizes, table, spectrum[j], grid)
    if tick == 0:
        gains = gains_of(sizes, layers, vel, wave_row(sizes, aux))
        columns = region[...].astype(F32).T
    for x in range(sx):
        raw = from_left(table("y"), grid[x])
        if tick == 0:
            g_re, g_im = gains(columns[:, x : x + 1], jnp.full((1, 1), float(x), F32), y_places(sizes))
            gain_re[x] = g_re
            gain_im[x] = g_im
        else:
            g_re, g_im = gain_re[x], gain_im[x]
        f_re, f_im = correct(raw[:, :sz], raw[:, sz:], g_re, g_im)
        field[0, x] = f_re.astype(BF16)
        field[1, x] = f_im.astype(BF16)


def last_kernel(tick, sizes, places, *refs):
    sx, sy, sz = sizes
    narrow, wide, symbol, gain_re, gain_im, from_west, south = refs[:7]
    fields = refs[7 : 7 + tick]
    out, south_hat, grid, field, sems = refs[7 + tick :]
    copies = []
    for i, earlier in enumerate(fields):
        copy = pltpu.make_async_copy(earlier, out.at[i], sems.at[i])
        copy.start()
        copies.append(copy)
    table = table_of(narrow, places[0])
    values = values_of(wide, places[1])
    transform_south(sizes, table, south, south_hat)
    blocks = [
        jnp.concatenate(spectrum_block(j, sizes, from_west[j], values, kept_pairs(j, sizes, symbol), south_hat), axis=0)
        for j in range(sy // SUB)
    ]
    for j in range(sy // SUB):
        invert_block(j, sizes, table, blocks[j], grid)
    for x in range(sx):
        raw = from_left(table("y"), grid[x])
        f_re, f_im = correct(raw[:, :sz], raw[:, sz:], gain_re[x], gain_im[x])
        field[0, x] = f_re.astype(BF16)
        field[1, x] = f_im.astype(BF16)
        if x % GROUP == GROUP - 1:
            span = pl.ds(x - GROUP + 1, GROUP)
            copy = pltpu.make_async_copy(field.at[:, span], out.at[tick, :, span], sems.at[len(copies)])
            copy.start()
            copies.append(copy)
    for copy in copies:
        copy.wait()


def call(kernel, name, args, out_shape, scratch, cost, in_specs=None, out_specs=None):
    vm = pl.BlockSpec(memory_space=pltpu.VMEM)
    return pl.pallas_call(
        kernel,
        out_shape=out_shape,
        in_specs=in_specs or [vm] * len(args),
        out_specs=out_specs or [vm] * len(out_shape),
        scratch_shapes=scratch,
        cost_estimate=pl.CostEstimate(flops=cost, bytes_accessed=4 << 20, transcendentals=0),
        compiler_params=pltpu.CompilerParams(vmem_limit_bytes=24 * 1024 * 1024),
        name=name,
    )(*args)


def local(west_in, south_in, region, pml_layers, vel_table, src_slot, src_cell, src_amp, wave_sq):
    sx, sy = region.shape
    sz = vel_table.shape[1]
    sizes = (sx, sy, sz)
    (narrow, narrow_at), (wide, wide_at), tall = constants(sx, sy, sz)
    places = (narrow_at, wide_at)
    shape = jax.ShapeDtypeStruct
    like = lambda a: shape(a.shape, a.dtype)
    vm = pl.BlockSpec(memory_space=pltpu.VMEM)
    west_hat = pltpu.VMEM((DEPTH, sy, 2 * sz), F32)
    south_hat = pltpu.VMEM((sx * (DEPTH + 1), 2 * sz), F32)
    hats = [south_hat, west_hat]
    west_shape = shape((sy // SUB, sx * SUB, 2 * sz), F32)
    grid = pltpu.VMEM((sx, sy, 2 * sz), F32)
    trace_shapes = [shape((2, DEPTH, sy, sz), F32), shape((2, sx * DEPTH, sz), F32)]
    spectrum_shape = shape((sy // SUB, 2 * sx * SUB, sz), F32)
    field_shape = shape((2, sx, sy, sz), BF16)
    symbol_shape = shape((2, sy // SUB, sx * SUB, sz), F32)
    gain_shapes = [shape((sx, sy, sz), F32)] * 2
    cost = 10**9

    south = south_in.reshape(2, sx * DEPTH, sz)
    tables = [jnp.asarray(t) for t in (narrow, wide, tall)]
    layers = pml_layers.reshape(1, 4)
    args = [tables[0], west_in, south, tables[1], src_slot, src_cell, src_amp, wave_sq.reshape(1, 1), tables[2]]
    args += [region, vel_table, layers]
    args = [pltpu.with_memory_space_constraint(a, pltpu.HBM) if a.size > 1 else a for a in args]
    moved = [west_in, south, src_slot, src_cell, src_amp, wave_sq.reshape(1, 1)]
    res = call(
        functools.partial(traces_kernel, 0, sizes, places),
        "traces0",
        args,
        trace_shapes
        + [spectrum_shape]
        + [like(t) for t in tables]
        + [shape((aux_rows(sizes), sz), F32)]
        + trace_shapes
        + [like(region), like(vel_table), like(layers)],
        hats + [west_hat] + [pltpu.VMEM(m.shape, m.dtype) for m in moved] + [pltpu.SemaphoreType.DMA((len(args),))],
        cost,
        in_specs=[pl.BlockSpec(memory_space=pltpu.HBM)] * len(args),
    )
    east, north, spectrum, narrow, wide, tall, aux, gain_east, gain_north, region, vel_table, layers = res
    fields = []
    gains = None
    for tick in range(1, TICKS):
        west = shift(east, "gx")
        south = shift(north, "gy")
        if tick == 1:
            given = [narrow, spectrum, aux, region, vel_table, layers, wide]
            results = [field_shape, *gain_shapes, symbol_shape]
        else:
            given = [narrow, spectrum, *gains]
            results = [field_shape]
        field, *made = call(
            functools.partial(field_kernel, tick - 1, sizes, places), f"field{tick - 1}", given, results, [grid], cost
        )
        if made:
            *gains, symbol = made
        fields.append(field)
        (from_west,) = call(
            functools.partial(west_kernel, tick, sizes, places),
            f"west{tick}",
            [narrow, aux, west, field],
            [west_shape],
            [west_hat, pltpu.VMEM((sx, 2 * sz), F32)],
            cost,
            in_specs=[vm, vm, vm, pl.BlockSpec(memory_space=pl.ANY)],
        )
        if tick + 1 < TICKS:
            east, north, spectrum = call(
                functools.partial(traces_kernel, tick, sizes, places),
                f"traces{tick}",
                [narrow, wide, tall, symbol, gain_east, gain_north, from_west, south],
                trace_shapes + [spectrum_shape],
                hats,
                cost,
            )
    given = [narrow, wide, symbol, *gains, from_west, south, *fields]
    (out,) = call(
        functools.partial(last_kernel, TICKS - 1, sizes, places),
        "last",
        given,
        [shape((TICKS, *field_shape.shape), BF16)],
        [south_hat, grid, pltpu.VMEM(field_shape.shape, BF16), pltpu.SemaphoreType.DMA((TICKS - 1 + sx // GROUP,))],
        cost,
        out_specs=[pl.BlockSpec(memory_space=pl.ANY)],
    )
    return out


def solution(mesh):
    in_specs = (
        P(None, "gx", "gy", None),
        P(None, "gx", "gy", None),
        P("gx", "gy"),
        P(None, "gx", "gy"),
        P(),
        P("gx", "gy"),
        P("gx", "gy"),
        P(),
        P(),
    )
    out_specs = P(None, None, "gx", "gy", None)
    return jax.shard_map(local, mesh=mesh, in_specs=in_specs, out_specs=out_specs, check_vma=False)
```

```python
import functools

import jax
import jax.numpy as jnp
import ml_dtypes
import numpy as np
from jax import lax
from jax.experimental import pallas as pl
from jax.experimental.pallas import tpu as pltpu
from jax.sharding import PartitionSpec as P

DEPTH = 4
TICKS = 3
SUB = 8
GROUP = 8
DAMPING = 0.25
PEAK = 4.0
BASE = 6.0
F32 = jnp.float32
BF16 = jnp.bfloat16


def shift(array, axis):
    peers = lax.axis_size(axis)
    return lax.ppermute(array, axis, [(i, i + 1) for i in range(peers - 1)])


def basis(n):
    k = np.arange(1, n + 1, dtype=np.float64)
    table = np.sqrt(2.0 / (n + 1)) * np.sin(np.pi * np.outer(k, k) / (n + 1))
    return table, 2.0 - 2.0 * np.cos(np.pi * k / (n + 1))


def halves(table):
    high = table.astype(ml_dtypes.bfloat16)
    low = (table - high.astype(np.float64)).astype(ml_dtypes.bfloat16)
    return high, low


def stacked(table):
    high, low = halves(table)
    return np.block([[high, high], [low, np.zeros_like(low)]])


def constants(sx, sy, sz):
    bx, ex = basis(sx)
    by, ey = basis(sy)
    bz, ez = basis(sz)
    zh, zl = halves(bz)
    half = sx // 2
    eye = np.eye(SUB)
    narrow = {
        "z": np.block([[zh, zl], [zh, zl]]),
        "even": stacked(np.kron(bx[:half, 0::2], eye)),
        "odd": stacked(np.kron(bx[:half, 1::2], eye)),
        "y": stacked(by),
        "south": stacked(np.kron(bx, np.eye(DEPTH))),
        "west": np.concatenate(halves(np.kron(bx[order(sx), :DEPTH], eye)), axis=1),
    }
    wide = {
        "eigen": ey[:, None] + ez[None, :],
        "bx": bx,
        "by": by,
        "bz": bz,
        "reach": np.repeat(by[:, :DEPTH].T.reshape(DEPTH * sy, 1), sz, axis=1),
    }
    east = halves(np.kron(bx[sx - DEPTH :, order(sx)], eye))
    north = []
    for j in range(sy // SUB):
        north += halves(np.kron(np.eye(sx)[:, order(sx)], by[sy - DEPTH :, j * SUB : (j + 1) * SUB]))
    traces = np.concatenate([*east, *north])
    return pack(narrow, ml_dtypes.bfloat16), pack(wide, np.float32), traces


def order(sx):
    return list(range(0, sx, 2)) + list(range(1, sx, 2))


def pack(tables, dtype):
    width = max(t.shape[1] for t in tables.values())
    rows, places, at = [], {}, 0
    for name, t in tables.items():
        places[name] = (at, t.shape)
        rows.append(np.pad(t.astype(np.float64), ((0, 0), (0, width - t.shape[1]))))
        at += t.shape[0]
    return np.concatenate(rows).astype(dtype), places


def split(values):
    high = values.astype(BF16)
    low = (values - high.astype(F32)).astype(BF16)
    return high, low


def dot(a, b):
    return jnp.dot(a, b, preferred_element_type=F32)


def along_z(rows, z_table):
    high, low = split(rows)
    both = dot(jnp.concatenate([high, low], axis=1), z_table)
    size_z = rows.shape[1]
    return both[:, :size_z] + both[:, size_z:]


def from_left(table, rows):
    high, low = split(rows)
    both = dot(table, jnp.concatenate([high, low], axis=0))
    n = both.shape[0] // 2
    return both[:n] + both[n:]


def ramp(layers, distance):
    portion = jnp.maximum(layers - distance, 0.0) / jnp.maximum(layers, 1.0)
    return portion * portion


def point_rows(sizes, values, slot, cell, amp, wave, aux):
    sx, sy, sz = sizes
    bits = [size.bit_length() - 1 for size in sizes]
    number = cell[...]
    cell_x = lax.shift_right_logical(number, bits[1] + bits[2])
    cell_y = lax.shift_right_logical(number, bits[2]) & (sy - 1)
    cell_z = number & (sz - 1)

    def column(name, size, where):
        lane = lax.broadcasted_iota(jnp.int32, (size, sz), 1)
        return jnp.sum(jnp.where(lane == where, values(name, 0, size), 0.0), axis=1, keepdims=True)

    aux[:sy] = jnp.broadcast_to(column("by", sy, cell_y), (sy, sz))
    row = lax.broadcasted_iota(jnp.int32, (sz, sz), 0)
    bz_row = jnp.sum(jnp.where(row == cell_z, values("bz", 0, sz), 0.0), axis=0, keepdims=True)
    aux[sy : sy + sx] = column("bx", sx, cell_x) * bz_row
    first = lax.axis_size("gx") + lax.axis_size("gy") - 2 - lax.axis_index("gx") - lax.axis_index("gy")
    lane = lax.broadcasted_iota(jnp.int32, amp.shape, 1)
    at = sy + sx
    for tick in range(TICKS):
        strength = jnp.sum(jnp.where(lane == first + tick, amp[...], 0.0), axis=1, keepdims=True)
        strength = jnp.where(slot[...] == first + tick, strength, 0.0)
        aux[at + 2 * tick : at + 2 * tick + 2] = jnp.broadcast_to(strength, (2, sz))
    at += 2 * TICKS
    aux[at : at + 1] = jnp.broadcast_to(wave[...], (1, sz))


def aux_rows(sizes):
    sx, sy, _ = sizes
    return -(-(sx + sy + 2 * TICKS + 1) // SUB) * SUB


def table_of(narrow, places):
    def table(name):
        at, shape = places[name]
        return narrow[at : at + shape[0], : shape[1]]

    return table


def values_of(wide, places):
    def values(name, start, size):
        at, shape = places[name]
        return wide[at + start : at + start + size, :]

    return values


def wave_row(sizes, aux):
    at = sizes[0] + sizes[1] + 2 * TICKS
    return aux[at : at + 1]


def spread_west(sizes, table, west, west_hat):
    sx, sy, sz = sizes
    rows = along_z(west[...].reshape(2 * DEPTH * sy, sz), table("z")).reshape(2, DEPTH, sy, sz)
    for d in range(DEPTH):
        west_hat[d] = from_left(table("y"), jnp.concatenate([rows[0, d], rows[1, d]], axis=1))
    n = DEPTH * SUB
    west_table = table("west")
    left = jnp.concatenate([west_table[:, :n], west_table[:, :n], west_table[:, n:]], axis=1)
    blocks = []
    for j in range(sy // SUB):
        high, low = split(west_hat[:, j * SUB : (j + 1) * SUB, :].reshape(n, 2 * sz))
        blocks.append(dot(left, jnp.concatenate([high, low, high], axis=0)))
    return blocks


def transform_south(sizes, table, south, south_hat):
    sx, _, sz = sizes
    n = DEPTH * sx
    rows = along_z(south[...].reshape(2 * n, sz), table("z")).reshape(2, n, sz)
    south_hat[:n] = from_left(table("south"), jnp.concatenate([rows[0], rows[1]], axis=1))


def place_point(tick, sizes, aux, point_hat):
    sx, sy, sz = sizes
    for c in range(2):
        row = sy + sx + 2 * tick + c
        point_hat[:, c * sz : (c + 1) * sz] = aux[sy : sy + sx] * aux[row : row + 1]


def inverse_symbol(j, sizes, values, aux):
    sx, _, sz = sizes
    eigen_x = [float(v) for v in basis(sx)[1].astype(np.float32)]
    w2 = wave_row(sizes, aux)
    damping = jnp.broadcast_to(-DAMPING * w2, (SUB, sz))
    damping_square = damping * damping
    base = values("eigen", j * SUB, SUB) - w2
    pairs = []
    for k in order(sx):
        shifted = base + eigen_x[k]
        size = shifted * shifted + damping_square
        inverse = pl.reciprocal(size, approx=True)
        inverse = inverse * (2.0 - size * inverse)
        pairs.append((shifted * inverse, damping * inverse))
    return pairs


def spectrum_block(j, sizes, coeffs, values, pairs, south_hat, point=None):
    sx, sy, sz = sizes
    reach = [values("reach", d * sy + j * SUB, SUB) for d in range(DEPTH)]
    if point is not None:
        reach.append(point)
    new_re = []
    new_im = []
    for i, k in enumerate(order(sx)):
        line = slice(i * SUB, (i + 1) * SUB)
        c_re = coeffs[line, :sz]
        c_im = coeffs[line, sz:]
        for d, factor in enumerate(reach):
            row = k * DEPTH + d if d < DEPTH else sx * DEPTH + k
            row = slice(row, row + 1)
            c_re += factor * south_hat[row, :sz]
            c_im += factor * south_hat[row, sz:]
        p, q = pairs[i]
        new_re.append(c_re * p + c_im * q)
        new_im.append(c_im * p - c_re * q)
    return jnp.concatenate(new_re, axis=0), jnp.concatenate(new_im, axis=0)


def kept_pairs(j, sizes, symbol):
    return [tuple(symbol[c, j, i * SUB : (i + 1) * SUB] for c in range(2)) for i in range(sizes[0])]


def invert_block(j, sizes, table, rows, grid):
    sx, _, sz = sizes
    half = sx // 2
    here = slice(j * SUB, (j + 1) * SUB)
    lines = along_z(rows, table("z"))
    n = half * SUB
    e = from_left(table("even"), jnp.concatenate([lines[:n], lines[2 * n : 3 * n]], axis=1))
    o = from_left(table("odd"), jnp.concatenate([lines[n : 2 * n], lines[3 * n :]], axis=1))
    grid[:half, here, :] = (e + o).reshape(half, SUB, 2 * sz)
    difference = e - o
    for x in range(half):
        grid[sx - 1 - x, here, :] = difference[x * SUB : (x + 1) * SUB]


def gains_of(sizes, layers, vel, w2):
    sx, sy, _ = sizes
    count = vel.shape[0]
    layer = [layers[:, i : i + 1].astype(F32) for i in range(4)]
    rows = jnp.concatenate(split(vel[...] - w2), axis=0)

    def gains(labels, x_pos, y_pos):
        n = labels.shape[0]
        lane = (lax.broadcasted_iota(jnp.int32, (n, 2 * count), 1) % count).astype(F32)
        contrast = dot((labels == lane).astype(BF16), rows)
        sigma = ramp(layer[0], x_pos) + ramp(layer[1], sx - 1.0 - x_pos)
        sigma = PEAK * (sigma + ramp(layer[2], y_pos) + ramp(layer[3], sy - 1.0 - y_pos))
        inverse = 1.0 / (BASE * BASE + sigma * sigma)
        return 1.0 + contrast * (BASE * inverse), -contrast * (sigma * inverse)

    return gains


def y_places(sizes):
    return lax.broadcasted_iota(jnp.int32, (sizes[1], 1), 0).astype(F32)


def correct(raw_re, raw_im, g_re, g_im):
    return raw_re * g_re - raw_im * g_im, raw_im * g_re + raw_re * g_im


def trace_gains(sizes, region, vel, layers, wave, gain_east, gain_north):
    sx, sy, _ = sizes
    n_north = DEPTH * sx
    gains = gains_of(sizes, layers, vel, wave[...])
    labels = region[...].astype(F32)
    columns = labels.T
    for d in range(DEPTH):
        x = sx - DEPTH + d
        g_re, g_im = gains(columns[:, x : x + 1], jnp.full((1, 1), float(x), F32), y_places(sizes))
        gain_east[0, d] = g_re
        gain_east[1, d] = g_im
    row = lax.broadcasted_iota(jnp.int32, (n_north, sx), 0)
    repeat = (row // DEPTH == lax.broadcasted_iota(jnp.int32, (n_north, sx), 1)).astype(BF16)
    spread = dot(repeat, labels.astype(BF16))
    row = lax.broadcasted_iota(jnp.int32, (n_north, sy), 0)
    lane = lax.broadcasted_iota(jnp.int32, (n_north, sy), 1)
    mine = jnp.sum(jnp.where(lane == sy - DEPTH + row % DEPTH, spread, 0.0), axis=1, keepdims=True)
    row = lax.broadcasted_iota(jnp.int32, (n_north, 1), 0)
    x_pos = (row // DEPTH).astype(F32)
    y_pos = (sy - DEPTH + row % DEPTH).astype(F32)
    g_re, g_im = gains(mine, x_pos, y_pos)
    gain_north[0] = g_re
    gain_north[1] = g_im


def traces_kernel(tick, sizes, places, *refs):
    sx, sy, sz = sizes
    refs = list(refs)
    take = lambda n: [refs.pop(0) for _ in range(n)]
    waits = []
    if tick == 0:
        fetched = take(12)
        fetched = fetched[4:8] + fetched[9:] + fetched[:4] + fetched[8:9]
        east, north, spectrum, narrow, wide, tall, aux, gain_east, gain_north, region, vel, layers = take(12)
    else:
        narrow, wide, tall, symbol, gain_east, gain_north, from_west, south = take(8)
        east, north, spectrum = take(3)
    south_hat, east_hat = take(2)
    if tick == 0:
        west_hat, west, south, slot, cell, amp, wave = take(7)
        (fetch_sems,) = take(1)
        targets = [slot, cell, amp, wave, region, vel, layers, narrow, west, south, wide, tall]
        for i, target in enumerate(targets):
            copy = pltpu.make_async_copy(fetched[i], target, fetch_sems.at[i])
            copy.start()
            waits.append(copy)
    table = table_of(narrow, places[0])
    values = values_of(wide, places[1])
    n_east = DEPTH * SUB
    n_north = DEPTH * sx
    if tick == 0:
        for copy in waits[:10]:
            copy.wait()
        starts = spread_west(sizes, table, west, west_hat)
    transform_south(sizes, table, south, south_hat)
    if tick == 0:
        for copy in waits[10:]:
            copy.wait()
        point_rows(sizes, values, slot, cell, amp, wave, aux)
        place_point(tick, sizes, aux, south_hat.at[DEPTH * sx :])
    else:
        starts = [from_west[j] for j in range(sy // SUB)]
    total = jnp.zeros((n_north, 2 * sz), F32)
    blocks = []
    for j in range(sy // SUB):
        pairs = inverse_symbol(j, sizes, values, aux) if tick == 0 else kept_pairs(j, sizes, symbol)
        point = aux[j * SUB : (j + 1) * SUB] if tick == 0 else None
        blocks.append(spectrum_block(j, sizes, starts[j], values, pairs, south_hat, point))
    for j in range(sy // SUB):
        here = slice(j * SUB, (j + 1) * SUB)
        re, im = blocks[j]
        n = re.shape[0]
        spectrum[j, :n] = re
        spectrum[j, n:] = im
        high, low = split(jnp.concatenate([re, im], axis=1))
        east_table = tall[: 2 * n_east]
        start = 2 * n_east + 2 * n_north * j
        north_table = tall[start : start + 2 * n_north]
        main = dot(jnp.concatenate([east_table, north_table], axis=0), high)
        rest = dot(jnp.concatenate([east_table[:n_east], north_table[:n_north]], axis=0), low)
        part = main[:n_east] + main[n_east : 2 * n_east] + rest[:n_east]
        east_hat[:, here, :] = part.reshape(DEPTH, SUB, 2 * sz)
        at = 2 * n_east
        total += main[at : at + n_north] + main[at + n_north :] + rest[n_east:]

    if tick == 0:
        trace_gains(sizes, region, vel, layers, wave, gain_east, gain_north)
    zt = table("z")
    planes = [from_left(table("y"), east_hat[d]) for d in range(DEPTH)]
    lines = [p[:, :sz] for p in planes] + [p[:, sz:] for p in planes]
    lines = along_z(jnp.concatenate(lines, axis=0), zt).reshape(2, DEPTH, sy, sz)
    east[0], east[1] = correct(lines[0], lines[1], gain_east[0], gain_east[1])
    rows = from_left(table("south"), total)
    lines = along_z(jnp.concatenate([rows[:, :sz], rows[:, sz:]], axis=0), zt)
    north[0], north[1] = correct(lines[:n_north], lines[n_north:], gain_north[0], gain_north[1])


def west_kernel(tick, sizes, places, narrow, aux, west, _, out, west_hat, point_hat):
    sx, _, sz = sizes
    place_point(tick, sizes, aux, point_hat)
    for j, block in enumerate(spread_west(sizes, table_of(narrow, places[0]), west, west_hat)):
        factor = aux[j * SUB : (j + 1) * SUB]
        for i, k in enumerate(order(sx)):
            line = slice(i * SUB, (i + 1) * SUB)
            for part in (slice(0, sz), slice(sz, 2 * sz)):
                out[j, line, part] = block[line, part] + factor * point_hat[k : k + 1, part]


def field_kernel(tick, sizes, places, *refs):
    sx, sy, sz = sizes
    refs = list(refs)
    take = lambda n: [refs.pop(0) for _ in range(n)]
    if tick == 0:
        narrow, spectrum, aux, region, vel, layers, wide = take(7)
        field, gain_re, gain_im, symbol = take(4)
        values = values_of(wide, places[1])
        for j in range(sy // SUB):
            for i, pair in enumerate(inverse_symbol(j, sizes, values, aux)):
                for c in range(2):
                    symbol[c, j, i * SUB : (i + 1) * SUB] = pair[c]
    else:
        narrow, spectrum, gain_re, gain_im = take(4)
        (field,) = take(1)
    (grid,) = take(1)
    table = table_of(narrow, places[0])
    for j in range(sy // SUB):
        invert_block(j, sizes, table, spectrum[j], grid)
    if tick == 0:
        gains = gains_of(sizes, layers, vel, wave_row(sizes, aux))
        columns = region[...].astype(F32).T
    for x in range(sx):
        raw = from_left(table("y"), grid[x])
        if tick == 0:
            g_re, g_im = gains(columns[:, x : x + 1], jnp.full((1, 1), float(x), F32), y_places(sizes))
            gain_re[x] = g_re
            gain_im[x] = g_im
        else:
            g_re, g_im = gain_re[x], gain_im[x]
        f_re, f_im = correct(raw[:, :sz], raw[:, sz:], g_re, g_im)
        field[0, x] = f_re.astype(BF16)
        field[1, x] = f_im.astype(BF16)


def last_kernel(tick, sizes, places, *refs):
    sx, sy, sz = sizes
    narrow, wide, symbol, gain_re, gain_im, from_west, south = refs[:7]
    fields = refs[7 : 7 + tick]
    out, south_hat, grid, field, sems = refs[7 + tick :]
    copies = []
    for i, earlier in enumerate(fields):
        copy = pltpu.make_async_copy(earlier, out.at[i], sems.at[i])
        copy.start()
        copies.append(copy)
    table = table_of(narrow, places[0])
    values = values_of(wide, places[1])
    transform_south(sizes, table, south, south_hat)
    blocks = [
        jnp.concatenate(spectrum_block(j, sizes, from_west[j], values, kept_pairs(j, sizes, symbol), south_hat), axis=0)
        for j in range(sy // SUB)
    ]
    for j in range(sy // SUB):
        invert_block(j, sizes, table, blocks[j], grid)
    for x in range(sx):
        raw = from_left(table("y"), grid[x])
        f_re, f_im = correct(raw[:, :sz], raw[:, sz:], gain_re[x], gain_im[x])
        field[0, x] = f_re.astype(BF16)
        field[1, x] = f_im.astype(BF16)
        if x % GROUP == GROUP - 1:
            span = pl.ds(x - GROUP + 1, GROUP)
            copy = pltpu.make_async_copy(field.at[:, span], out.at[tick, :, span], sems.at[len(copies)])
            copy.start()
            copies.append(copy)
    for copy in copies:
        copy.wait()


def call(kernel, name, args, out_shape, scratch, cost, in_specs=None, out_specs=None):
    vm = pl.BlockSpec(memory_space=pltpu.VMEM)
    return pl.pallas_call(
        kernel,
        out_shape=out_shape,
        in_specs=in_specs or [vm] * len(args),
        out_specs=out_specs or [vm] * len(out_shape),
        scratch_shapes=scratch,
        cost_estimate=pl.CostEstimate(flops=cost, bytes_accessed=4 << 20, transcendentals=0),
        compiler_params=pltpu.CompilerParams(vmem_limit_bytes=24 * 1024 * 1024),
        name=name,
    )(*args)


def local(west_in, south_in, region, pml_layers, vel_table, src_slot, src_cell, src_amp, wave_sq):
    sx, sy = region.shape
    sz = vel_table.shape[1]
    sizes = (sx, sy, sz)
    (narrow, narrow_at), (wide, wide_at), tall = constants(sx, sy, sz)
    places = (narrow_at, wide_at)
    shape = jax.ShapeDtypeStruct
    like = lambda a: shape(a.shape, a.dtype)
    vm = pl.BlockSpec(memory_space=pltpu.VMEM)
    west_hat = pltpu.VMEM((DEPTH, sy, 2 * sz), F32)
    south_hat = pltpu.VMEM((sx * (DEPTH + 1), 2 * sz), F32)
    hats = [south_hat, west_hat]
    west_shape = shape((sy // SUB, sx * SUB, 2 * sz), F32)
    grid = pltpu.VMEM((sx, sy, 2 * sz), F32)
    trace_shapes = [shape((2, DEPTH, sy, sz), F32), shape((2, sx * DEPTH, sz), F32)]
    spectrum_shape = shape((sy // SUB, 2 * sx * SUB, sz), F32)
    field_shape = shape((2, sx, sy, sz), BF16)
    symbol_shape = shape((2, sy // SUB, sx * SUB, sz), F32)
    gain_shapes = [shape((sx, sy, sz), F32)] * 2
    cost = 10**9

    south = south_in.reshape(2, sx * DEPTH, sz)
    tables = [jnp.asarray(t) for t in (narrow, wide, tall)]
    layers = pml_layers.reshape(1, 4)
    args = [tables[0], west_in, south, tables[1], src_slot, src_cell, src_amp, wave_sq.reshape(1, 1), tables[2]]
    args += [region, vel_table, layers]
    args = [pltpu.with_memory_space_constraint(a, pltpu.HBM) if a.size > 1 else a for a in args]
    moved = [west_in, south, src_slot, src_cell, src_amp, wave_sq.reshape(1, 1)]
    res = call(
        functools.partial(traces_kernel, 0, sizes, places),
        "traces0",
        args,
        trace_shapes
        + [spectrum_shape]
        + [like(t) for t in tables]
        + [shape((aux_rows(sizes), sz), F32)]
        + trace_shapes
        + [like(region), like(vel_table), like(layers)],
        hats + [west_hat] + [pltpu.VMEM(m.shape, m.dtype) for m in moved] + [pltpu.SemaphoreType.DMA((len(args),))],
        cost,
        in_specs=[pl.BlockSpec(memory_space=pltpu.HBM)] * len(args),
    )
    east, north, spectrum, narrow, wide, tall, aux, gain_east, gain_north, region, vel_table, layers = res
    fields = []
    gains = None
    for tick in range(1, TICKS):
        west = shift(east, "gx")
        south = shift(north, "gy")
        if tick == 1:
            given = [narrow, spectrum, aux, region, vel_table, layers, wide]
            results = [field_shape, *gain_shapes, symbol_shape]
        else:
            given = [narrow, spectrum, *gains]
            results = [field_shape]
        field, *made = call(
            functools.partial(field_kernel, tick - 1, sizes, places), f"field{tick - 1}", given, results, [grid], cost
        )
        if made:
            *gains, symbol = made
        fields.append(field)
        (from_west,) = call(
            functools.partial(west_kernel, tick, sizes, places),
            f"west{tick}",
            [narrow, aux, west, field],
            [west_shape],
            [west_hat, pltpu.VMEM((sx, 2 * sz), F32)],
            cost,
            in_specs=[vm, vm, vm, pl.BlockSpec(memory_space=pl.ANY)],
        )
        if tick + 1 < TICKS:
            east, north, spectrum = call(
                functools.partial(traces_kernel, tick, sizes, places),
                f"traces{tick}",
                [narrow, wide, tall, symbol, gain_east, gain_north, from_west, south],
                trace_shapes + [spectrum_shape],
                hats,
                cost,
            )
    given = [narrow, wide, symbol, *gains, from_west, south, *fields]
    (out,) = call(
        functools.partial(last_kernel, TICKS - 1, sizes, places),
        "last",
        given,
        [shape((TICKS, *field_shape.shape), BF16)],
        [south_hat, grid, pltpu.VMEM(field_shape.shape, BF16), pltpu.SemaphoreType.DMA((TICKS - 1 + sx // GROUP,))],
        cost,
        out_specs=[pl.BlockSpec(memory_space=pl.ANY)],
    )
    return out


def solution(mesh):
    in_specs = (
        P(None, "gx", "gy", None),
        P(None, "gx", "gy", None),
        P("gx", "gy"),
        P(None, "gx", "gy"),
        P(),
        P("gx", "gy"),
        P("gx", "gy"),
        P(),
        P(),
    )
    out_specs = P(None, None, "gx", "gy", None)
    return jax.shard_map(local, mesh=mesh, in_specs=in_specs, out_specs=out_specs, check_vma=False)
```
